32 devices in a mesh: section: 4 (over x, core), doc: 2 (over y), mp: 4 (over z).
Axes of the slice: x: 2, y: 2, z: 4, core: 2. Of those that a mesh axis runs over, the one named last changes fastest.
Arguments:
- queries: bfloat16 [4, 512, 8, 4, 128], P('doc', None, 'section', 'mp'), may hold values from -420 to 420
- cotangent: bfloat16 [4, 512, 8, 4, 128], P('doc', None, 'section', 'mp'), may hold values from -180 to 180
- cache: bfloat16 [32, 128, 4, 2, 128], P('doc', 'section', 'mp'), may hold values from -7 to 7
- momentum: float32 [32, 128, 4, 2, 128], P('doc', 'section', 'mp'), may hold values from -3 to 3
- doc_lists: int32 [4, 8], P('doc'), may hold values from 0 to 31, as said below
- place: int32 [32], replicated, may hold values from 0 to 31, as said below
Outputs:
- attention: bfloat16 [4, 512, 8, 4, 128], P('doc', None, 'section', 'mp')
- new_cache: bfloat16 [32, 128, 4, 2, 128], P('doc', 'section', 'mp')
- new_momentum: float32 [32, 128, 4, 2, 128], P('doc', 'section', 'mp')
The draws below stay inside these ranges and needn't reach their ends.
Inputs may be any that keep to these rules, and one draw needn't show every extreme that they name: `doc_lists`: the 2 rows of one index of doc (an aligned block of rows) name 16 different documents in all. Counting each document's owner as place[document] // 16, those documents lie on at most 8 per owner. `place`: each row of cache holds exactly one document.
All inputs are finite; a program needn't handle non-finite values.
Results may differ from the reference program's by a relative error of at most 0.017.
Values may be sent and summed in bfloat16 or wider, within the bound.
A program may use at most 64 MiB of HBM per device.

```python
import math
import jax
import jax.numpy as jnp
from jax import lax

HD = 128
GROUP = 8
KVH = 4
LEN = 128
SEQ = 512
ROWS_DEV = 2
LIST = 8
DOC_DEV = 16
ROWS = 4
DOCS = 32
N_SECTION = 4


def make_place(key):
    return jax.random.permutation(jax.random.fold_in(key, 11), DOCS).astype(jnp.int32)


def make_lists(key):
    place = make_place(key)
    inverse = jnp.argsort(place, stable=True).astype(jnp.int32)
    owners = DOCS // DOC_DEV
    readers = ROWS // ROWS_DEV
    request_total = ROWS_DEV * LIST
    owner_used = min(owners, request_total)
    shared_offset = jax.random.randint(jax.random.fold_in(key, 43), (owners,), 0, DOC_DEV, dtype=jnp.int32)

    def per_reader(reader_key, reader):
        key_a, key_b, key_c, key_d, key_e = jax.random.split(reader_key, 5)
        owner_ids = jnp.arange(owners, dtype=jnp.int32)
        random_part = jax.random.randint(key_a, (owners,), 0, 65536, dtype=jnp.int32)
        owner_lean = owner_ids * (32768 // owners)
        special = reader < 2
        target_doc = jnp.where(reader == 0, DOCS - 1, 0).astype(jnp.int32)
        target_place = place[target_doc]
        drawn_forced = owners - 1 - jax.random.randint(key_b, (), 0, max(1, owners // 4), dtype=jnp.int32)
        forced = jnp.where(special, target_place // DOC_DEV, drawn_forced).astype(jnp.int32)
        owner_score = (random_part + owner_lean) * owners + owner_ids
        owner_score = jnp.where(owner_ids == forced, 1073741824, owner_score)
        chosen = lax.top_k(owner_score, owner_used)[1].astype(jnp.int32)
        popular = jax.random.randint(key_c, (owners,), 0, 4, dtype=jnp.int32) < 3
        own_offset = jax.random.randint(key_e, (owners,), 0, DOC_DEV, dtype=jnp.int32)
        offset = jnp.where(popular, shared_offset, own_offset)
        offset = jnp.where(special & (owner_ids == forced), target_place % DOC_DEV, offset).astype(jnp.int32)
        request_ids = jnp.arange(request_total, dtype=jnp.int32)
        owner_pick = chosen[request_ids % owner_used]
        slot_index = (offset[owner_pick] + request_ids // owner_used) % DOC_DEV
        doc_ids = inverse[owner_pick * DOC_DEV + slot_index]
        shuffle = jax.random.permutation(key_d, request_total)
        return doc_ids[shuffle]
    reader_keys = jax.random.split(jax.random.fold_in(key, 41), readers)
    reader_index = jnp.arange(readers, dtype=jnp.int32)
    return jax.vmap(per_reader)(reader_keys, reader_index).reshape(ROWS, LIST).astype(jnp.int32)


def cache_values(key):
    normal_part = jnp.clip(jax.random.normal(jax.random.fold_in(key, 21), (DOCS, LEN, KVH, 2, HD), jnp.float32), -6.0, 6.0)
    return normal_part


def draw_place(key, part):
    return make_place(key)


def draw_doc_lists(key, part):
    return make_lists(key)


def draw_cache(key, part):
    return cache_values(key).astype(jnp.bfloat16)


def draw_cotangent(key, part):
    noise = jnp.clip(jax.random.normal(jax.random.fold_in(key, 51), (ROWS, SEQ, GROUP, KVH, HD), jnp.float32), -6.0, 6.0)
    values = 30.0 * noise
    return values.astype(jnp.bfloat16)


def draw_queries(key, part):
    values = jnp.clip(jax.random.normal(jax.random.fold_in(key, 31), (ROWS, SEQ, GROUP, KVH, HD), jnp.float32), -6.0, 6.0)
    return values.astype(jnp.bfloat16)


def block_scale(rng, extent, cuts, least, top_value):
    def one(position, shards_of):
        steps = jax.random.uniform(jax.random.fold_in(jax.random.fold_in(rng, 6), position), (shards_of,), jnp.float32, least / len(cuts), top_value / len(cuts))
        return jnp.repeat(jnp.exp(steps), extent[position] // shards_of).reshape((-1,) + (1,) * (len(extent) - position - 1))

    gain = one(*cuts[0])
    for cut in cuts[1:]:
        gain = gain * one(*cut)
    return gain


def gaussian(rng, shape, deviation, reach, shards=(), kind=jnp.bfloat16):
    gain = block_scale(rng, shape, shards, -0.22, 0.18) if shards else 1.0
    values = jax.random.normal(rng, shape, jnp.float32) * deviation * gain
    return jnp.minimum(jnp.maximum(values, -reach), reach).astype(kind)


def setup_inputs(seed: int = 0) -> dict:
    arg_keys = jax.random.split(jax.random.key(seed), 7)
    return {
        "queries": draw_queries(jax.random.fold_in(arg_keys[6], 71), 0),
        "cotangent": draw_cotangent(jax.random.fold_in(arg_keys[6], 71), 0),
        "cache": draw_cache(jax.random.fold_in(arg_keys[6], 71), 0),
        "momentum": gaussian(arg_keys[3], (DOCS, LEN, KVH, 2, HD), 0.5, 3.0, ((0, 2), (1, 4), (2, 4)), jnp.float32),
        "doc_lists": draw_doc_lists(jax.random.fold_in(arg_keys[6], 71), 0),
        "place": draw_place(jax.random.fold_in(arg_keys[6], 71), 0),
    }


momentum_decay = 0.9
step_rate = 0.3
clip_level = 0.5

def reference(queries, cotangent, cache, momentum, doc_lists, place):
    score_scale = 1.0 / math.sqrt(HD)
    pair_count = GROUP // N_SECTION
    positions = place[doc_lists].astype(jnp.int32)

    def row_step(grad_sum, operands):
        query_row, tangent_row, cache_rows = operands
        memory = cache[cache_rows]
        key_rows = memory[:, :, :, 0, :].reshape(LIST * LEN, KVH, HD).astype(jnp.float32)
        value_rows = memory[:, :, :, 1, :].reshape(LIST * LEN, KVH, HD).astype(jnp.float32)
        query_full = query_row.astype(jnp.float32)
        tangent_full = tangent_row.astype(jnp.float32)
        scores = jnp.einsum('sgkd,nkd->sgkn', query_full, key_rows) * score_scale
        weights = jax.nn.softmax(scores, axis=-1)
        weight_bf = lax.optimization_barrier(weights.astype(jnp.bfloat16)).astype(jnp.float32)
        attended = jnp.einsum('sgkn,nkd->sgkd', weight_bf, value_rows).astype(jnp.bfloat16)
        row_delta = lax.optimization_barrier(jnp.sum(attended.astype(jnp.float32) * tangent_full, axis=-1, keepdims=True))
        grad_weights = jnp.einsum('sgkd,nkd->sgkn', tangent_full, value_rows)
        grad_scores = (weights * (grad_weights - row_delta) * score_scale).astype(jnp.bfloat16)
        grad_scores = lax.optimization_barrier(grad_scores).astype(jnp.float32)
        block_shape = (SEQ, N_SECTION, pair_count, KVH, LIST * LEN)
        head_shape = (SEQ, N_SECTION, pair_count, KVH, HD)
        grad_keys = jnp.einsum('sbpkn,sbpkd->bnkd', grad_scores.reshape(block_shape), query_full.reshape(head_shape))
        grad_values = jnp.einsum('sbpkn,sbpkd->bnkd', weight_bf.reshape(block_shape), tangent_full.reshape(head_shape))
        blocks = jnp.stack([grad_keys, grad_values], axis=3)
        blocks = lax.optimization_barrier(blocks.astype(jnp.bfloat16)).astype(jnp.float32)
        contribution = lax.optimization_barrier(jnp.sum(blocks, axis=0)).reshape(LIST, LEN, KVH, 2, HD)
        return (grad_sum.at[cache_rows].add(contribution), attended)
    start = jnp.zeros((DOCS, LEN, KVH, 2, HD), jnp.float32)
    gradient, attention = lax.scan(row_step, start, (queries, cotangent, positions))
    norm_value = jnp.sqrt(jnp.sum(gradient * gradient))
    clip_limit = clip_level * math.sqrt(DOCS * LEN * KVH * 2 * HD)
    factor = clip_limit / jnp.maximum(norm_value, clip_limit)
    new_momentum = momentum_decay * momentum + factor * gradient
    new_cache = (cache.astype(jnp.float32) - step_rate * new_momentum).astype(jnp.bfloat16)
    return (attention, new_cache, new_momentum)
```

```python
import functools
import math

import jax
import jax.numpy as jnp
from jax import lax
from jax.experimental import pallas as pl
from jax.experimental.pallas import tpu as pltpu
from jax.sharding import PartitionSpec as P

momentum_decay = 0.9
step_rate = 0.3
clip_level = 0.5
MESH = pl.DeviceIdType.MESH


def nt(a, b):
    return lax.dot_general(a, b, (((1,), (1,)), ((), ())), preferred_element_type=jnp.float32)


def mm(a, b):
    return jnp.dot(a, b, preferred_element_type=jnp.float32)


def kernel(
    cfg,
    lists_ref, place_ref, q_ref, t_ref, cache_ref, mom_ref,
    att_ref, newc_ref, newm_ref,
    mypos, allpos, tab, target, inverse,
    posvm, wide, kvc, arr, outbuf, keys, vals, valt, dk, dv,
    keep, snd, rcv, parcel, ret, part1, part2,
    pos_send, pos_recv, loc_sem, dir_send, arr_recv, fwd_send,
    sib_send, sib_recv, ret_send, ret_recv, n1_send, n1_recv, n2_send, n2_recv,
):
    sections, owners, mps, cap, doc_dev, len_part, rows, list_len, clip_limit, score_scale = cfg
    low = 2 if sections % 2 == 0 else 1
    high = sections // low
    requests = rows * list_len
    head = q_ref.shape[-1]
    sec = lax.axis_index("section")
    doc = lax.axis_index("doc")
    mp = lax.axis_index("mp")
    hi = sec // low
    lo = sec % low

    def rot(base, step, size):
        return lax.rem(base + step, size)

    group = [(a, b) for a in range(sections) for b in range(owners) if (a, b) != (0, 0)]
    peers = [(a, b) for a in range(high) for b in range(owners) if (a, b) != (0, 0)]
    barrier = pltpu.get_barrier_semaphore()
    for a, b in group:
        pl.semaphore_signal(
            barrier, inc=1,
            device_id={"section": rot(sec, a, sections), "doc": rot(doc, b, owners), "mp": mp},
            device_id_type=MESH,
        )
    for c in range(1, mps):
        pl.semaphore_signal(
            barrier, inc=1, device_id={"section": sec, "doc": doc, "mp": rot(mp, c, mps)},
            device_id_type=MESH,
        )

    def to(s, d):
        return {"section": s, "doc": d, "mp": mp}

    def remote(src, dst, ssem, rsem, dev):
        return pltpu.make_async_remote_copy(
            src_ref=src, dst_ref=dst, send_sem=ssem, recv_sem=rsem, device_id=dev,
            device_id_type=MESH,
        )

    count = doc_dev * len_part
    wide[0 : 2 * count, :] = cache_ref[...].astype(jnp.float32)
    kvc[:, 0] = wide[pl.ds(0, count, stride=2), :].astype(jnp.bfloat16).reshape(doc_dev, len_part, head)
    kvc[:, 1] = wide[pl.ds(1, count, stride=2), :].astype(jnp.bfloat16).reshape(doc_dev, len_part, head)

    lane = lax.broadcasted_iota(jnp.int32, (8, 128), 1)
    vec = jnp.zeros((8, 128), jnp.int32)
    places = []
    for r in range(requests):
        where = place_ref[lists_ref[r // list_len, r % list_len]]
        places.append(where)
        vec = jnp.where(lane == r, where, vec)
    posvm[doc] = vec

    def slots(get, d):
        found = [jnp.int32(-1)] * cap
        seen = jnp.int32(0)
        for r in range(requests):
            where = get(r)
            mine = (where // doc_dev) == doc
            local = where % doc_dev
            for c in range(min(cap, r + 1)):
                found[c] = jnp.where(mine & (seen == c), local, found[c])
            seen = seen + mine.astype(jnp.int32)
        for c in range(cap):
            tab[d * cap + c] = found[c]
        return found

    pl.semaphore_wait(barrier, len(group) + mps - 1)

    pos_copies = []
    for b in range(1, owners):
        cp = remote(posvm.at[doc], posvm.at[doc], pos_send.at[b], pos_recv.at[doc], to(sec, rot(doc, b, owners)))
        cp.start()
        pos_copies.append(cp)

    sends = []
    sib = hi * low + rot(lo, 1, low)

    def block(s, d):
        return arr.at[s, pl.ds(d * cap, cap)]

    def forward(h, d):
        if low == 1:
            return
        s = h * low + lo
        cp = remote(block(s, d), block(s, d), fwd_send.at[h, d], arr_recv.at[s, d], to(sib, doc))
        cp.start()
        sends.append(cp)

    found = slots(lambda r: places[r], doc)
    for c in range(cap):
        arr[sec, doc * cap + c] = kvc[jnp.maximum(found[c], 0)]
    for a in range(1, high):
        h = rot(hi, a, high)
        cp = remote(block(sec, doc), block(sec, doc), dir_send.at[a, 0], arr_recv.at[sec, doc], to(h * low + lo, doc))
        cp.start()
        sends.append(cp)
    forward(hi, doc)

    for b in range(1, owners):
        d = rot(doc, b, owners)
        remote(posvm.at[d], posvm.at[d], pos_send.at[b], pos_recv.at[d], to(sec, d)).wait_recv()
        local = pltpu.make_async_copy(posvm.at[d], allpos.at[d], loc_sem)
        local.start()
        local.wait()
        found = slots(lambda r: allpos[d, 0, r], d)
        for c in range(cap):
            outbuf[b, c] = kvc[jnp.maximum(found[c], 0)]
        for a in range(high):
            h = rot(hi, a, high)
            cp = remote(outbuf.at[b], block(sec, doc), dir_send.at[a, b], arr_recv.at[sec, doc], to(h * low + lo, d))
            cp.start()
            sends.append(cp)

    targets = []
    for r in range(requests):
        rank = jnp.int32(0)
        for e in range(r):
            rank = rank + ((places[e] // doc_dev) == (places[r] // doc_dev)).astype(jnp.int32)
        targets.append((places[r] // doc_dev) * cap + rank)
        target[r] = targets[r]
    for i in range(owners * cap):
        who = jnp.int32(0)
        for r in range(requests):
            who = jnp.where(targets[r] == i, r, who)
        inverse[i] = who

    for a, b in peers:
        h, d = rot(hi, a, high), rot(doc, b, owners)
        s = h * low + lo
        remote(block(s, d), block(s, d), dir_send.at[a, b], arr_recv.at[s, d], to(s, d)).wait_recv()
        forward(h, d)
    if low > 1:
        for a in range(high):
            for b in range(owners):
                h, d = rot(hi, a, high), rot(doc, b, owners)
                s = h * low + rot(lo, 1, low)
                remote(block(s, d), block(s, d), fwd_send.at[h, d], arr_recv.at[s, d], to(s, d)).wait_recv()

    seq = q_ref.shape[1]
    tile = 256 if seq % 256 == 0 else seq
    exp_scale = score_scale * math.log2(math.e)
    shape5 = (list_len, high, low, len_part, head)
    key_count = list_len * sections * len_part
    for row in range(rows):
        for i in range(list_len):
            slot = target[row * list_len + i]
            for s in range(sections):
                at = (i * sections + s) * len_part
                piece = arr[s, slot]
                keys[at : at + len_part, :] = piece[0]
                vals[at : at + len_part, :] = piece[1]
        valt[...] = vals[...].T
        dk[...] = jnp.zeros_like(dk)
        dv[...] = jnp.zeros_like(dv)

        def step(j, carry):
            at = pl.ds(pl.multiple_of(j * tile, tile), tile)
            q = q_ref[row, at, :]
            t = t_ref[row, at, :]
            scores = nt(keys[...], q)
            top = jnp.max(scores, axis=0, keepdims=True)
            power = jnp.exp2((scores - top) * exp_scale)
            weights = power * (1.0 / jnp.sum(power, axis=0, keepdims=True))
            weight_bf = weights.astype(jnp.bfloat16)
            attended = mm(valt[...], weight_bf).astype(jnp.bfloat16).astype(jnp.float32)
            att_ref[row, at, :] = attended.T.astype(jnp.bfloat16)
            delta = jnp.sum(attended * t.astype(jnp.float32).T, axis=0, keepdims=True)
            grad = (weights * (nt(vals[...], t) - delta)).astype(jnp.bfloat16)
            dk[...] += mm(grad, q).reshape(shape5)
            dv[...] += mm(weight_bf, t).reshape(shape5)
            return carry

        lax.fori_loop(0, seq // tile, step, 0)
        span = pl.ds(row * list_len, list_len)
        for h in range(high):
            keep[span, h, 0] = dk[:, h, lo] * score_scale
            keep[span, h, 1] = dv[:, h, lo]
            if low > 1:
                snd[span, h, 0] = (dk[:, h, rot(lo, 1, low)] * score_scale).astype(jnp.bfloat16)
                snd[span, h, 1] = dv[:, h, rot(lo, 1, low)].astype(jnp.bfloat16)
        if low > 1:
            cp = remote(snd.at[span], rcv.at[span], sib_send.at[row], sib_recv.at[row], to(sib, doc))
            cp.start()
            sends.append(cp)

    if low > 1:
        for row in range(rows):
            span = pl.ds(row * list_len, list_len)
            remote(snd.at[span], rcv.at[span], sib_send.at[row], sib_recv.at[row], to(sib, doc)).wait_recv()

    def total(request, h):
        value = keep[request, h]
        if low > 1:
            value = value + rcv[request, h].astype(jnp.float32)
        return value.astype(jnp.bfloat16)

    def slot_block(h, d):
        return ret.at[h, pl.ds(d * cap, cap)]

    for a, b in peers[::-1]:
        h, d = rot(hi, a, high), rot(doc, b, owners)
        for c in range(cap):
            parcel[a, b, c] = total(inverse[d * cap + c], h)
        cp = remote(parcel.at[a, b], slot_block(hi, doc), ret_send.at[a, b], ret_recv.at[hi, doc], to(h * low + lo, d))
        cp.start()
        sends.append(cp)
    for c in range(cap):
        ret[hi, doc * cap + c] = total(inverse[doc * cap + c], hi)
    for a, b in peers:
        h, d = rot(hi, a, high), rot(doc, b, owners)
        remote(parcel.at[a, b], slot_block(h, d), ret_send.at[a, b], ret_recv.at[h, d], to(h * low + lo, d)).wait_recv()

    def gather(p, square):
        value = jnp.zeros((2, len_part, head), jnp.float32)
        for d in range(owners):
            pick = jnp.int32(0)
            named = jnp.float32(0.0)
            for c in range(cap):
                same = tab[d * cap + c] == p
                pick = jnp.where(same, c, pick)
                named = jnp.where(same, jnp.float32(1.0), named)
            both = ret[0, d * cap + pick].astype(jnp.float32)
            for h in range(1, high):
                both = both + ret[h, d * cap + pick].astype(jnp.float32)
            value = value + jnp.where(named > 0.5, both, 0.0)
        base = p * 2 * len_part
        wide[pl.ds(base, len_part, stride=2), :] = value[0]
        wide[pl.ds(base + 1, len_part, stride=2), :] = value[1]
        return square + jnp.sum((value * value).reshape(-1, 8, head), axis=0)

    square = lax.fori_loop(0, doc_dev, gather, jnp.zeros((8, head), jnp.float32))

    part1[sec * owners + doc] = square
    for n, (a, b) in enumerate(group):
        s, d = rot(sec, a, sections), rot(doc, b, owners)
        mine = part1.at[sec * owners + doc]
        cp = remote(mine, mine, n1_send.at[n], n1_recv.at[sec * owners + doc], to(s, d))
        cp.start()
        sends.append(cp)
    for n, (a, b) in enumerate(group):
        s, d = rot(sec, a, sections), rot(doc, b, owners)
        other = part1.at[s * owners + d]
        remote(other, other, n1_send.at[n], n1_recv.at[s * owners + d], to(s, d)).wait_recv()
    part2[mp] = jnp.sum(part1[...], axis=0)
    for c in range(1, mps):
        cp = remote(part2.at[mp], part2.at[mp], n2_send.at[c], n2_recv.at[mp], {"section": sec, "doc": doc, "mp": rot(mp, c, mps)})
        cp.start()
        sends.append(cp)
    for c in range(1, mps):
        m = rot(mp, c, mps)
        remote(part2.at[m], part2.at[m], n2_send.at[c], n2_recv.at[m], {"section": sec, "doc": doc, "mp": m}).wait_recv()
    whole = jnp.sum(part2[...], axis=0)
    whole = jnp.sum(jnp.sum(whole, axis=0, keepdims=True), axis=1, keepdims=True)
    factor = clip_limit / jnp.maximum(jnp.sqrt(whole), clip_limit)
    fresh = momentum_decay * mom_ref[...] + factor * wide[0 : 2 * count, :]
    newm_ref[...] = fresh
    newc_ref[...] = (cache_ref[...].astype(jnp.float32) - step_rate * fresh).astype(jnp.bfloat16)
    for cp in pos_copies + sends:
        cp.wait_send()


def body(queries, cotangent, cache, momentum, doc_lists, place):
    rows, seq_len, heads, kv_count, head = queries.shape
    doc_dev, len_part = cache.shape[:2]
    doc_total = place.shape[0]
    owners = doc_total // doc_dev
    sections = lax.axis_size("section")
    mps = lax.axis_size("mp")
    list_len = doc_lists.shape[1]
    requests = rows * list_len
    used = min(owners, requests)
    cap = (requests + used - 1) // used
    low = 2 if sections % 2 == 0 else 1
    high = sections // low
    entry_count = doc_total * len_part * sections * kv_count * mps * 2 * head
    clip_limit = clip_level * math.sqrt(entry_count)
    cfg = (sections, owners, mps, cap, doc_dev, len_part, rows, list_len, clip_limit, 1.0 / math.sqrt(head))
    f32, bf16, i32 = jnp.float32, jnp.bfloat16, jnp.int32
    key_count = list_len * sections * len_part
    flat = 2 * doc_dev * len_part
    vm, dma = pltpu.VMEM, pltpu.SemaphoreType.DMA
    shape5 = (list_len, high, low, len_part, head)
    piece = (2, len_part, head)
    vmem = pl.BlockSpec(memory_space=pltpu.VMEM)
    smem = pl.BlockSpec(memory_space=pltpu.SMEM)
    queries_flat = queries.reshape(rows, seq_len * heads, head)
    att, newc, newm = pl.pallas_call(
        functools.partial(kernel, cfg),
        out_shape=(
            jax.ShapeDtypeStruct(queries_flat.shape, bf16),
            jax.ShapeDtypeStruct((flat, head), bf16),
            jax.ShapeDtypeStruct((flat, head), f32),
        ),
        in_specs=[smem, smem, vmem, vmem, vmem, vmem],
        out_specs=(vmem, vmem, vmem),
        scratch_shapes=[
            pltpu.SMEM((requests,), i32),
            pltpu.SMEM((owners, 8, 128), i32),
            pltpu.SMEM((owners * cap,), i32),
            pltpu.SMEM((requests,), i32),
            pltpu.SMEM((owners * cap,), i32),
            vm((owners, 8, 128), i32),
            vm((flat + 8, head), f32),
            vm((doc_dev,) + piece, bf16),
            vm((sections, owners * cap) + piece, bf16),
            vm((owners, cap) + piece, bf16),
            vm((key_count, head), bf16),
            vm((key_count, head), bf16),
            vm((head, key_count), bf16),
            vm(shape5, f32),
            vm(shape5, f32),
            vm((requests, high) + piece, f32),
            vm((requests, high) + piece, bf16),
            vm((requests, high) + piece, bf16),
            vm((high, owners, cap) + piece, bf16),
            vm((high, owners * cap) + piece, bf16),
            vm((sections * owners, 8, head), f32),
            vm((mps, 8, head), f32),
            dma((owners,)),
            dma((owners,)),
            dma,
            dma((high, owners)),
            dma((sections, owners)),
            dma((high, owners)),
            dma((rows,)),
            dma((rows,)),
            dma((high, owners)),
            dma((high, owners)),
            dma((sections * owners,)),
            dma((sections * owners,)),
            dma((mps,)),
            dma((mps,)),
        ],
        compiler_params=pltpu.CompilerParams(
            collective_id=0, has_side_effects=True, vmem_limit_bytes=48 * 1024 * 1024
        ),
        cost_estimate=pl.CostEstimate(
            flops=10 * rows * seq_len * heads * key_count * head,
            bytes_accessed=4 * 1024 * 1024,
            transcendentals=rows * seq_len * heads * key_count,
        ),
    )(
        doc_lists,
        place,
        queries_flat,
        cotangent.reshape(queries_flat.shape),
        cache.reshape(flat, head),
        momentum.reshape(flat, head),
    )
    return att.reshape(queries.shape), newc.reshape(cache.shape), newm.reshape(momentum.shape)


def solution(mesh):
    in_specs = (
        P("doc", None, "section", "mp", None),
        P("doc", None, "section", "mp", None),
        P("doc", "section", "mp", None, None),
        P("doc", "section", "mp", None, None),
        P("doc", None),
        P(),
    )
    out_specs = (
        P("doc", None, "section", "mp", None),
        P("doc", "section", "mp", None, None),
        P("doc", "section", "mp", None, None),
    )
    return jax.shard_map(body, mesh=mesh, in_specs=in_specs, out_specs=out_specs, check_vma=False)
```

```python
import functools
import math

import jax
import jax.numpy as jnp
from jax import lax
from jax.experimental import pallas as pl
from jax.experimental.pallas import tpu as pltpu
from jax.sharding import PartitionSpec as P

momentum_decay = 0.9
step_rate = 0.3
clip_level = 0.5
MESH = pl.DeviceIdType.MESH


def nt(a, b):
    return lax.dot_general(a, b, (((1,), (1,)), ((), ())), preferred_element_type=jnp.float32)


def mm(a, b):
    return jnp.dot(a, b, preferred_element_type=jnp.float32)


def kernel(
    cfg,
    lists_ref, place_ref, q_hbm, t_hbm, cache_hbm, mom_hbm,
    att_hbm, newc_ref, newm_ref,
    allpos, tab, target, inverse,
    q_ref, t_ref, att_ref, cache_ref, mom_ref,
    posvm, wide, kvc, arr_k, arr_v, outbuf, keys, vals, valt, wts, dkv,
    keep, snd, rcv_k, rcv_v, parcel, ret, parts,
    in_sem, out_sem, pos_send, pos_recv, loc_sem, dir_send, arr_recv, fwd_send,
    sib_send, sib_recv, ret_send, ret_recv, n_send, n_recv,
):
    sections, owners, mps, cap, doc_dev, len_part, rows, list_len, clip_limit, score_scale = cfg
    arr, rcv = (arr_k, arr_v), (rcv_k, rcv_v)
    low = 2 if sections % 2 == 0 else 1
    high = sections // low
    requests = rows * list_len
    head = q_ref.shape[-1]
    sec = lax.axis_index("section")
    doc = lax.axis_index("doc")
    mp = lax.axis_index("mp")
    hi = sec // low
    lo = sec % low
    everyone = sections * owners * mps
    me = (sec * owners + doc) * mps + mp

    def rot(base, step, size):
        return lax.rem(base + step, size)

    def device(n):
        return {"section": n // (owners * mps), "doc": (n // mps) % owners, "mp": n % mps}

    peers = [(a, b) for a in range(high) for b in range(owners) if (a, b) != (0, 0)]
    loads = [
        pltpu.make_async_copy(src, dst, in_sem.at[n])
        for n, (src, dst) in enumerate(
            ((cache_hbm, cache_ref), (q_hbm, q_ref), (t_hbm, t_ref), (mom_hbm, mom_ref))
        )
    ]
    leaves = [
        pltpu.make_async_copy(att_ref.at[row], att_hbm.at[row], out_sem.at[row]) for row in range(rows)
    ]
    loads[0].start()
    barrier = pltpu.get_barrier_semaphore()

    def greet(n, carry):
        pl.semaphore_signal(barrier, inc=1, device_id=device(rot(me, n, everyone)), device_id_type=MESH)
        return carry

    lax.fori_loop(1, everyone, greet, 0)
    for load in loads[1:]:
        load.start()

    def to(s, d):
        return {"section": s, "doc": d, "mp": mp}

    def remote(src, dst, ssem, rsem, dev):
        return pltpu.make_async_remote_copy(
            src_ref=src, dst_ref=dst, send_sem=ssem, recv_sem=rsem, device_id=dev,
            device_id_type=MESH,
        )

    lane = lax.broadcasted_iota(jnp.int32, (8, 128), 1)
    vec = jnp.zeros((8, 128), jnp.int32)
    places = []
    for r in range(requests):
        where = place_ref[lists_ref[r // list_len, r % list_len]]
        places.append(where)
        vec = jnp.where(lane == r, where, vec)
    posvm[doc] = vec

    def slots(get, d):
        found = [jnp.int32(-1)] * cap
        seen = jnp.int32(0)
        for r in range(requests):
            where = get(r)
            mine = (where // doc_dev) == doc
            local = where % doc_dev
            for c in range(min(cap, r + 1)):
                found[c] = jnp.where(mine & (seen == c), local, found[c])
            seen = seen + mine.astype(jnp.int32)
        for c in range(cap):
            tab[d * cap + c] = found[c]
        return found

    found = slots(lambda r: places[r], doc)

    loads[0].wait()
    count = doc_dev * len_part
    wide[0 : 2 * count, :] = cache_ref[...].astype(jnp.float32)
    for kv in range(2):
        kvc[kv] = wide[pl.ds(kv, count, stride=2), :].astype(jnp.bfloat16).reshape(doc_dev, len_part, head)
    for kv in range(2):
        for c in range(cap):
            arr[kv][sec, doc * cap + c] = kvc[kv, jnp.maximum(found[c], 0)]

    pl.semaphore_wait(barrier, everyone - 1)

    sends = []

    def send(src, dst, ssem, rsem, dev):
        cp = remote(src, dst, ssem, rsem, dev)
        cp.start()
        sends.append(cp)

    for b in range(1, owners):
        send(posvm.at[doc], posvm.at[doc], pos_send.at[b], pos_recv.at[doc], to(sec, rot(doc, b, owners)))

    sib = hi * low + rot(lo, 1, low)

    def block(kv, s, d):
        return arr[kv].at[s, pl.ds(d * cap, cap)]

    def forward(kv, h, d):
        if low == 1:
            return
        s = h * low + lo
        send(block(kv, s, d), block(kv, s, d), fwd_send.at[kv, h, d], arr_recv.at[kv, s, d], to(sib, doc))

    def arrive(kv, s, d):
        remote(block(kv, s, d), block(kv, s, d), dir_send.at[kv, 0, 0], arr_recv.at[kv, s, d], to(s, d)).wait_recv()

    for kv in range(2):
        for a in range(1, high):
            h = rot(hi, a, high)
            send(block(kv, sec, doc), block(kv, sec, doc), dir_send.at[kv, a, 0], arr_recv.at[kv, sec, doc], to(h * low + lo, doc))
    for kv in range(2):
        forward(kv, hi, doc)

    for b in range(1, owners):
        d = rot(doc, b, owners)
        remote(posvm.at[d], posvm.at[d], pos_send.at[b], pos_recv.at[d], to(sec, d)).wait_recv()
        local = pltpu.make_async_copy(posvm.at[d], allpos.at[d], loc_sem)
        local.start()
        local.wait()
        found = slots(lambda r: allpos[d, 0, r], d)
        for kv in range(2):
            for c in range(cap):
                outbuf[kv, b, c] = kvc[kv, jnp.maximum(found[c], 0)]
            for a in range(high):
                h = rot(hi, a, high)
                send(outbuf.at[kv, b], block(kv, sec, doc), dir_send.at[kv, a, b], arr_recv.at[kv, sec, doc], to(h * low + lo, d))

    targets = []
    for r in range(requests):
        rank = jnp.int32(0)
        for e in range(r):
            rank = rank + ((places[e] // doc_dev) == (places[r] // doc_dev)).astype(jnp.int32)
        targets.append((places[r] // doc_dev) * cap + rank)
        target[r] = targets[r]
    for i in range(owners * cap):
        who = jnp.int32(0)
        for r in range(requests):
            who = jnp.where(targets[r] == i, r, who)
        inverse[i] = who

    def relay(kv):
        for a, b in peers:
            h, d = rot(hi, a, high), rot(doc, b, owners)
            arrive(kv, h * low + lo, d)
            forward(kv, h, d)

    def relayed(kv):
        if low > 1:
            for a in range(high):
                for b in range(owners):
                    arrive(kv, rot(hi, a, high) * low + rot(lo, 1, low), rot(doc, b, owners))

    def assemble(kv, row, dst):
        for i in range(list_len):
            slot = target[row * list_len + i]
            for s in range(sections):
                at = (i * sections + s) * len_part
                dst[at : at + len_part, :] = arr[kv][s, slot]

    exp_scale = score_scale * math.log2(math.e)
    shape5 = (list_len, high, low, len_part, head)

    def share(kv, row, value):
        dkv[kv] = value.reshape(shape5)
        span = pl.ds(row * list_len, list_len)
        for h in range(high):
            keep[kv, span, h] = dkv[kv, :, h, lo]
            if low > 1:
                snd[kv, span, h] = dkv[kv, :, h, rot(lo, 1, low)].astype(jnp.bfloat16)
        if low > 1:
            send(snd.at[kv, span], rcv[kv].at[span], sib_send.at[kv, row], sib_recv.at[kv, row], to(sib, doc))

    def slot_block(kv, h, d):
        return ret.at[kv, h, pl.ds(d * cap, cap)]

    def give_back(kv):
        if low > 1:
            for row in range(rows):
                span = pl.ds(row * list_len, list_len)
                remote(snd.at[kv, span], rcv[kv].at[span], sib_send.at[kv, row], sib_recv.at[kv, row], to(sib, doc)).wait_recv()

        def total(request, h):
            value = keep[kv, request, h]
            if low > 1:
                value = value + rcv[kv][request, h].astype(jnp.float32)
            return value.astype(jnp.bfloat16)

        for a, b in peers[::-1]:
            h, d = rot(hi, a, high), rot(doc, b, owners)
            for c in range(cap):
                parcel[kv, a, b, c] = total(inverse[d * cap + c], h)
            send(parcel.at[kv, a, b], slot_block(kv, hi, doc), ret_send.at[kv, a, b], ret_recv.at[kv, hi, doc], to(h * low + lo, d))
        for c in range(cap):
            ret[kv, hi, doc * cap + c] = total(inverse[doc * cap + c], hi)

    def first_half(row):
        assemble(0, row, keys.at[row])
        scores = nt(keys[row], q_ref[row])
        top = jnp.max(scores, axis=0, keepdims=True)
        power = jnp.exp2((scores - top) * exp_scale)
        weights = power * (1.0 / jnp.sum(power, axis=0, keepdims=True))
        wts[row] = weights.astype(jnp.bfloat16)
        share(1, row, mm(wts[row], t_ref[row]))

    def second_half(row):
        assemble(1, row, vals)
        valt[...] = vals[...].T
        t = t_ref[row]
        attended = mm(valt[...], wts[row]).astype(jnp.bfloat16).astype(jnp.float32)
        att_ref[row] = attended.T.astype(jnp.bfloat16)
        leaves[row].start()
        delta = jnp.sum(attended * t.astype(jnp.float32).T, axis=0, keepdims=True)
        grad = (wts[row].astype(jnp.float32) * (nt(vals[...], t) - delta)).astype(jnp.bfloat16)
        share(0, row, mm(grad, q_ref[row]) * score_scale)

    relay(0)
    for load in loads[1:]:
        load.wait()
    relayed(0)
    for row in range(rows):
        first_half(row)
        if row == 0:
            relay(1)
    relayed(1)
    for row in range(rows):
        second_half(row)
        if row == 0:
            give_back(1)
    give_back(0)
    for kv in (1, 0):
        for a, b in peers:
            h, d = rot(hi, a, high), rot(doc, b, owners)
            remote(parcel.at[kv, a, b], slot_block(kv, h, d), ret_send.at[kv, a, b], ret_recv.at[kv, h, d], to(h * low + lo, d)).wait_recv()

    def gather(p, square):
        base = p * 2 * len_part
        value = [jnp.zeros((len_part, head), jnp.float32)] * 2
        for d in range(owners):
            pick = jnp.int32(0)
            named = jnp.float32(0.0)
            for c in range(cap):
                same = tab[d * cap + c] == p
                pick = jnp.where(same, c, pick)
                named = jnp.where(same, jnp.float32(1.0), named)
            for kv in range(2):
                both = ret[kv, 0, d * cap + pick].astype(jnp.float32)
                for h in range(1, high):
                    both = both + ret[kv, h, d * cap + pick].astype(jnp.float32)
                value[kv] = value[kv] + jnp.where(named > 0.5, both, 0.0)
        for kv in range(2):
            wide[pl.ds(base + kv, len_part, stride=2), :] = value[kv]
            square = square + jnp.sum((value[kv] * value[kv]).reshape(-1, 8, head), axis=0)
        return square

    square = lax.fori_loop(0, doc_dev, gather, jnp.zeros((8, head), jnp.float32))

    parts[me] = square

    def tell(n, carry):
        remote(parts.at[me], parts.at[me], n_send.at[n], n_recv.at[me], device(rot(me, n, everyone))).start()
        return carry

    def hear(n, carry):
        other = rot(me, n, everyone)
        remote(parts.at[other], parts.at[other], n_send.at[n], n_recv.at[other], device(other)).wait_recv()
        return carry

    def told(n, carry):
        remote(parts.at[me], parts.at[me], n_send.at[n], n_recv.at[me], device(rot(me, n, everyone))).wait_send()
        return carry

    lax.fori_loop(1, everyone, tell, 0)
    newm_ref[...] = momentum_decay * mom_ref[...]
    for cp in sends:
        cp.wait_send()
    for leave in leaves:
        leave.wait()
    lax.fori_loop(1, everyone, hear, 0)
    whole = jnp.sum(parts[...], axis=0)
    whole = jnp.sum(jnp.sum(whole, axis=0, keepdims=True), axis=1, keepdims=True)
    factor = clip_limit / jnp.maximum(jnp.sqrt(whole), clip_limit)
    fresh = newm_ref[...] + factor * wide[0 : 2 * count, :]
    newm_ref[...] = fresh
    newc_ref[...] = (cache_ref[...].astype(jnp.float32) - step_rate * fresh).astype(jnp.bfloat16)
    lax.fori_loop(1, everyone, told, 0)


def body(queries, cotangent, cache, momentum, doc_lists, place):
    rows, seq_len, heads, kv_count, head = queries.shape
    doc_dev, len_part = cache.shape[:2]
    doc_total = place.shape[0]
    owners = doc_total // doc_dev
    sections = lax.axis_size("section")
    mps = lax.axis_size("mp")
    list_len = doc_lists.shape[1]
    requests = rows * list_len
    used = min(owners, requests)
    cap = (requests + used - 1) // used
    low = 2 if sections % 2 == 0 else 1
    high = sections // low
    entry_count = doc_total * len_part * sections * kv_count * mps * 2 * head
    clip_limit = clip_level * math.sqrt(entry_count)
    cfg = (sections, owners, mps, cap, doc_dev, len_part, rows, list_len, clip_limit, 1.0 / math.sqrt(head))
    f32, bf16, i32 = jnp.float32, jnp.bfloat16, jnp.int32
    key_count = list_len * sections * len_part
    flat = 2 * doc_dev * len_part
    vm, dma = pltpu.VMEM, pltpu.SemaphoreType.DMA
    shape5 = (list_len, high, low, len_part, head)
    piece = (len_part, head)
    everyone = sections * owners * mps
    hbm = pl.BlockSpec(memory_space=pltpu.HBM)
    vmem = pl.BlockSpec(memory_space=pltpu.VMEM)
    smem = pl.BlockSpec(memory_space=pltpu.SMEM)
    queries_flat = queries.reshape(rows, seq_len * heads, head)
    att, newc, newm = pl.pallas_call(
        functools.partial(kernel, cfg),
        out_shape=(
            jax.ShapeDtypeStruct(queries_flat.shape, bf16),
            jax.ShapeDtypeStruct((flat, head), bf16),
            jax.ShapeDtypeStruct((flat, head), f32),
        ),
        in_specs=[smem, smem, hbm, hbm, hbm, hbm],
        out_specs=(hbm, vmem, vmem),
        scratch_shapes=[
            pltpu.SMEM((owners, 8, 128), i32),
            pltpu.SMEM((owners * cap,), i32),
            pltpu.SMEM((requests,), i32),
            pltpu.SMEM((owners * cap,), i32),
            vm(queries_flat.shape, bf16),
            vm(queries_flat.shape, bf16),
            vm(queries_flat.shape, bf16),
            vm((flat, head), bf16),
            vm((flat, head), f32),
            vm((owners, 8, 128), i32),
            vm((flat + 8, head), f32),
            vm((2, doc_dev) + piece, bf16),
            vm((sections, owners * cap) + piece, bf16),
            vm((sections, owners * cap) + piece, bf16),
            vm((2, owners, cap) + piece, bf16),
            vm((rows, key_count, head), bf16),
            vm((key_count, head), bf16),
            vm((head, key_count), bf16),
            vm((rows, key_count, seq_len * heads), bf16),
            vm((2,) + shape5, f32),
            vm((2, requests, high) + piece, f32),
            vm((2, requests, high) + piece, bf16),
            vm((requests, high) + piece, bf16),
            vm((requests, high) + piece, bf16),
            vm((2, high, owners, cap) + piece, bf16),
            vm((2, high, owners * cap) + piece, bf16),
            vm((everyone, 8, head), f32),
            dma((4,)),
            dma((rows,)),
            dma((owners,)),
            dma((owners,)),
            dma,
            dma((2, high, owners)),
            dma((2, sections, owners)),
            dma((2, high, owners)),
            dma((2, rows)),
            dma((2, rows)),
            dma((2, high, owners)),
            dma((2, high, owners)),
            dma((everyone,)),
            dma((everyone,)),
        ],
        compiler_params=pltpu.CompilerParams(
            collective_id=0, has_side_effects=True, vmem_limit_bytes=56 * 1024 * 1024
        ),
        cost_estimate=pl.CostEstimate(
            flops=10 * rows * seq_len * heads * key_count * head,
            bytes_accessed=4 * 1024 * 1024,
            transcendentals=rows * seq_len * heads * key_count,
        ),
    )(
        doc_lists,
        place,
        queries_flat,
        cotangent.reshape(queries_flat.shape),
        cache.reshape(flat, head),
        momentum.reshape(flat, head),
    )
    return att.reshape(queries.shape), newc.reshape(cache.shape), newm.reshape(momentum.shape)


def solution(mesh):
    in_specs = (
        P("doc", None, "section", "mp", None),
        P("doc", None, "section", "mp", None),
        P("doc", "section", "mp", None, None),
        P("doc", "section", "mp", None, None),
        P("doc", None),
        P(),
    )
    out_specs = (
        P("doc", None, "section", "mp", None),
        P("doc", "section", "mp", None, None),
        P("doc", "section", "mp", None, None),
    )
    return jax.shard_map(body, mesh=mesh, in_specs=in_specs, out_specs=out_specs, check_vma=False)
```
